32 devices in a mesh: parts: 2 (over x), row: 4 (over y, core), col: 4 (over z).
Axes of the slice: x: 2, y: 2, z: 4, core: 2. Of those that a mesh axis runs over, the one named last changes fastest.
Arguments:
- pair: bfloat16 [192, 96, 128], P(('parts', 'row'), 'col'), parts along dimension 0, may hold values from -6 to 6
- atom_feats: bfloat16 [3072, 128], P(('parts', 'row', 'col')), parts along dimension 0, may hold values from -6 to 6
- atom_token: int32 [3072], P(('parts', 'row', 'col')), parts along dimension 0, may hold values from 0 to 95, never falling along the last dimension, each value on 1 to 32 neighbouring positions
- atom_mask: int32 [3072], P(('parts', 'row', 'col')), parts along dimension 0, may hold values 0 or 1
- token_mask: int32 [192], P('parts'), parts along dimension 0, may hold values 0 or 1
- w_atom: bfloat16 [128, 384], replicated, may hold values from -0.5 to 0.5
- gain_single: float32 [384], replicated, may hold values from 0.25 to 1.75
- w_rows: bfloat16 [384, 128], replicated, may hold values from -0.3125 to 0.3125
- w_cols: bfloat16 [384, 128], replicated, may hold values from -0.3125 to 0.3125
- gain_pair: float32 [128], replicated, may hold values from 0.25 to 1.75
- w_left: bfloat16 [128, 128], replicated, may hold values from -0.5 to 0.5
- w_left_gate: bfloat16 [128, 128], replicated, may hold values from -0.5 to 0.5
- w_right: bfloat16 [128, 128], replicated, may hold values from -0.5 to 0.5
- w_right_gate: bfloat16 [128, 128], replicated, may hold values from -0.5 to 0.5
- w_out_gate: bfloat16 [128, 128], replicated, may hold values from -0.5 to 0.5
- gain_tri: float32 [128], replicated, may hold values from 0.25 to 1.75
- w_out: bfloat16 [128, 128], replicated, may hold values from -0.5 to 0.5
- gain_trans: float32 [128], replicated, may hold values from 0.25 to 1.75
- w_up: bfloat16 [128, 512], replicated, may hold values from -0.5 to 0.5
- w_upgate: bfloat16 [128, 512], replicated, may hold values from -0.5 to 0.5
- w_down: bfloat16 [512, 128], replicated, may hold values from -0.25 to 0.25
Outputs:
- pair_out: bfloat16 [192, 96, 128], P(('parts', 'row'), 'col'), parts along dimension 0
The draws below stay inside these ranges and needn't reach their ends.
There are 2 independent parts, one for each index of `parts`. The reference program is written for one: setup_inputs(seed, part) draws one part's arguments, and reference() takes and returns one part's arrays. A program takes and returns all parts, laid end to end along the dimension named above; an argument that names none is the same for every part. Nothing has to cross between parts.
Inputs may be any that keep to these rules, and one draw needn't show every extreme that they name: `atom_token`: never falls along the atoms; every token has 1 to 32 atoms, and some token exactly 32.
All inputs are finite; a program needn't handle non-finite values. No bound on the sum of `atom_mask` on one device may be relied on, other than what follows from the above.
Results may differ from the reference program's by a relative error of at most 0.005.
Values may be sent and summed in bfloat16 or wider, within the bound.
A program may use at most 128 MiB of HBM per device.

```python
import math
import jax
import jax.numpy as jnp
import numpy as np
from jax import lax

CA = 128
CS = 384
CP = 128
HID = 512
MOST = 32
TOKENS = 96
ATOMS = 1536
ROWS_BLK = 24


def touch_ends(result, rng, smallest, top_value):
    extent = result.shape
    index_at = [jax.random.randint(jax.random.fold_in(rng, axis), (), 0, extent[axis]) for axis in range(len(extent))]
    result = result.at[tuple(index_at)].set(smallest)
    longest = extent.index(max(extent))
    index_at[longest] = (index_at[longest] + 1) % extent[longest]
    return result.at[tuple(index_at)].set(top_value)


def steps_of(own_key, extent, split, low, high):
    factor_of, own = 1.0, jax.random.fold_in(own_key, 6)
    for dim, shards_of in split:
        heights = jnp.exp(jax.random.uniform(jax.random.fold_in(own, dim), (shards_of,), jnp.float32, low / len(split), high / len(split)))
        factor_of = factor_of * jnp.repeat(heights, extent[dim] // shards_of).reshape([-1 if axis == dim else 1 for axis in range(len(extent))])
    return factor_of


def split_up(amount, total, most, lean):
    portions = [(1 << 20) // math.isqrt(rank ** lean) + 1 for rank in range(2, amount + 1)]
    spare, counts = total - most - (amount - 1), [1] * (amount - 1)
    while spare > 0:
        free = [i for i in range(amount - 1) if counts[i] < most]
        mass, left = sum([portions[i] for i in free]), spare
        for i in free:
            more = min(most - counts[i], max(1, left * portions[i] // mass), spare)
            counts[i] = counts[i] + more
            spare = spare - more
    return np.array([most] + counts)


def uneven(rng, number_of, total, bound, lean):
    if number_of == 2:
        one = jax.random.randint(rng, (), max(1, total - bound), min(bound, total - 1) + 1)
        return jnp.stack([one, total - one])
    tallies = jnp.asarray(split_up(number_of, total, bound, lean), jnp.int32)
    pairs = (number_of - 1) // 2
    source_of, sink = tallies[1:1 + 2 * pairs:2], tallies[2:2 + 2 * pairs:2]
    room = jnp.minimum(source_of - 1, bound - sink)
    shifted = jax.random.randint(jax.random.fold_in(rng, 1), (pairs,), 0, 1 << 20) % (room + 1)
    tallies = tallies.at[1:1 + 2 * pairs:2].set(source_of - shifted).at[2:2 + 2 * pairs:2].set(sink + shifted)
    return tallies[jax.random.permutation(jax.random.fold_in(rng, 2), number_of)]


def bell_draw(own_key, extent, width, reach, pieces=(), kind=jnp.bfloat16):
    loudness = steps_of(own_key, extent, pieces, -0.22, 0.18) if pieces else 1.0
    array = jax.random.normal(own_key, extent, jnp.float32) * width * loudness
    return jnp.minimum(jnp.maximum(array, -reach), reach).astype(kind)


def setup_inputs(seed: int = 0, part: int = 0) -> dict:
    keys = jax.random.split(jax.random.key(seed), 22)
    part_keys = jax.random.split(jax.random.fold_in(keys[21], part), 22)
    pair = bell_draw(part_keys[0], (TOKENS, TOKENS, CP), 1.0, 6.0, ((0, 4), (1, 4)))
    atom_feats = bell_draw(part_keys[1], (ATOMS, CA), 1.0, 6.0, ((0, 16),))
    atom_token = jnp.searchsorted(jnp.cumsum(uneven(part_keys[2], TOKENS, ATOMS, MOST, 2)), jnp.arange(ATOMS), side="right").astype(jnp.int32)
    atom_mask = touch_ends((jax.random.randint(part_keys[3], (ATOMS,), 0, 8) < 7).astype(jnp.int32), jax.random.fold_in(part_keys[3], 1), 0, 1)
    token_mask = touch_ends((jax.random.randint(part_keys[4], (TOKENS,), 0, 16) < 15).astype(jnp.int32), jax.random.fold_in(part_keys[4], 1), 0, 1)
    w_atom = bell_draw(keys[5], (CA, CS), CA ** -0.5, 0.5)
    gain_single = jnp.clip(1.0 + 0.15 * jax.random.normal(keys[6], (CS,), jnp.float32), 0.25, 1.75)
    w_rows = bell_draw(keys[7], (CS, CP), CS ** -0.5, 0.3125)
    w_cols = bell_draw(keys[8], (CS, CP), CS ** -0.5, 0.3125)
    gain_pair = jnp.clip(1.0 + 0.15 * jax.random.normal(keys[9], (CP,), jnp.float32), 0.25, 1.75)
    w_left = bell_draw(keys[10], (CP, CP), CP ** -0.5, 0.5)
    w_left_gate = bell_draw(keys[11], (CP, CP), CP ** -0.5, 0.5)
    w_right = bell_draw(keys[12], (CP, CP), CP ** -0.5, 0.5)
    w_right_gate = bell_draw(keys[13], (CP, CP), CP ** -0.5, 0.5)
    w_out_gate = bell_draw(keys[14], (CP, CP), CP ** -0.5, 0.5)
    gain_tri = jnp.clip(1.0 + 0.15 * jax.random.normal(keys[15], (CP,), jnp.float32), 0.25, 1.75)
    w_out = bell_draw(keys[16], (CP, CP), CP ** -0.5, 0.5)
    gain_trans = jnp.clip(1.0 + 0.15 * jax.random.normal(keys[17], (CP,), jnp.float32), 0.25, 1.75)
    w_up = bell_draw(keys[18], (CP, HID), CP ** -0.5, 0.5)
    w_upgate = bell_draw(keys[19], (CP, HID), CP ** -0.5, 0.5)
    w_down = bell_draw(keys[20], (HID, CP), HID ** -0.5, 0.25)
    return dict(pair=pair, atom_feats=atom_feats, atom_token=atom_token, atom_mask=atom_mask, token_mask=token_mask, w_atom=w_atom, gain_single=gain_single, w_rows=w_rows, w_cols=w_cols, gain_pair=gain_pair, w_left=w_left, w_left_gate=w_left_gate, w_right=w_right, w_right_gate=w_right_gate, w_out_gate=w_out_gate, gain_tri=gain_tri, w_out=w_out, gain_trans=gain_trans, w_up=w_up, w_upgate=w_upgate, w_down=w_down)


norm_epsilon = 1e-05

def layer_norm(values, gain_vec):
    centre = lax.optimization_barrier(jnp.mean(values, axis=-1, keepdims=True))
    centered = values - centre
    variance = lax.optimization_barrier(jnp.mean(centered * centered, axis=-1, keepdims=True))
    return centered * lax.rsqrt(variance + norm_epsilon) * gain_vec

def gated_proj(values, w_value, w_gate, pair_weight):
    gate_part = jax.nn.sigmoid(jnp.dot(values, w_gate, preferred_element_type=jnp.float32))
    value_part = jnp.dot(values, w_value, preferred_element_type=jnp.float32)
    return (gate_part * value_part * pair_weight[..., None]).astype(jnp.bfloat16)

def reference(pair, atom_feats, atom_token, atom_mask, token_mask, w_atom, gain_single, w_rows, w_cols, gain_pair, w_left, w_left_gate, w_right, w_right_gate, w_out_gate, gain_tri, w_out, gain_trans, w_up, w_upgate, w_down):
    highest = lax.Precision.HIGHEST
    member = (jnp.arange(TOKENS, dtype=jnp.int32)[:, None] == atom_token[None, :]).astype(jnp.float32)
    member = member * atom_mask.astype(jnp.float32)[None, :]
    projected = jnp.dot(atom_feats, w_atom, preferred_element_type=jnp.float32)
    pooled = jnp.dot(member, projected, precision=highest)
    single = layer_norm(pooled, gain_single)
    row_term = jnp.dot(single, w_rows.astype(jnp.float32), precision=highest)
    col_term = jnp.dot(single, w_cols.astype(jnp.float32), precision=highest)
    z_first = pair.astype(jnp.float32) + row_term[:, None, :] + col_term[None, :, :]
    normed_pair = layer_norm(z_first, gain_pair).astype(jnp.bfloat16)
    mask_all = token_mask.astype(jnp.float32)
    pair_weight = mask_all[:, None] * mask_all[None, :]
    left = gated_proj(normed_pair, w_left, w_left_gate, pair_weight).astype(jnp.float32)
    right = gated_proj(normed_pair, w_right, w_right_gate, pair_weight).astype(jnp.float32)

    def row_block(block_index):
        offset = (block_index * ROWS_BLK).astype(jnp.int32)
        left_block = lax.dynamic_slice_in_dim(left, offset, ROWS_BLK, 1)
        triangle = jnp.einsum('kic,kjc->ijc', left_block, right, precision=highest)
        first_rows = lax.dynamic_slice_in_dim(z_first, offset, ROWS_BLK, 0)
        normed_rows = lax.dynamic_slice_in_dim(normed_pair, offset, ROWS_BLK, 0)
        out_gate = jax.nn.sigmoid(jnp.dot(normed_rows, w_out_gate, preferred_element_type=jnp.float32))
        tri_normed = layer_norm(triangle, gain_tri).astype(jnp.bfloat16)
        z_second = first_rows + jnp.dot(tri_normed, w_out, preferred_element_type=jnp.float32) * out_gate
        trans_in = layer_norm(z_second, gain_trans).astype(jnp.bfloat16)
        hidden = (jax.nn.silu(jnp.dot(trans_in, w_upgate, preferred_element_type=jnp.float32)) * jnp.dot(trans_in, w_up, preferred_element_type=jnp.float32)).astype(jnp.bfloat16)
        return (z_second + jnp.dot(hidden, w_down, preferred_element_type=jnp.float32)).astype(jnp.bfloat16)
    blocks = lax.map(row_block, jnp.arange(TOKENS // ROWS_BLK, dtype=jnp.int32))
    return blocks.reshape(TOKENS, TOKENS, CP)
```

```python
import functools

import jax
import jax.numpy as jnp
from jax import lax
from jax.experimental import pallas as pl
from jax.experimental.pallas import tpu as pltpu
from jax.sharding import PartitionSpec as P

norm_epsilon = 1e-05
MESH = pl.DeviceIdType.MESH
SUM_TYPE = jnp.bfloat16


def layer_norm(values, gain_vec):
    centre = jnp.mean(values, axis=-1, keepdims=True)
    centered = values - centre
    variance = jnp.mean(centered * centered, axis=-1, keepdims=True)
    return centered * lax.rsqrt(variance + norm_epsilon) * gain_vec


def sigmoid(v):
    return 0.5 * jnp.tanh(0.5 * v) + 0.5


def mm(a, b):
    return jnp.dot(a, b, preferred_element_type=jnp.float32)


def mm_split(a, b):
    high = a.astype(jnp.bfloat16)
    low = (a - high.astype(jnp.float32)).astype(jnp.bfloat16)
    return mm(high, b) + mm(low, b)


def kernel(
    nrow, ncol, rb, cb, tokens,
    pair, feats, atom_token, atom_mask, token_mask,
    w_atom, gain_single, w_rows, w_cols, gain_pair,
    w_left, w_left_gate, w_right, w_right_gate, w_out_gate,
    gain_tri, w_out, gain_trans, w_up, w_upgate, w_down,
    out,
    feats_v, w_atom_v, w_rows_v, w_cols_v, w_l_v, w_r_v, w_og_v, w_out_v, w_up_v, w_ug_v, w_dn_v,
    left_pair, right_pair, part_sum, recv_row, col_sum, recv_col,
    row_term, col_term, left_blk, right_blk, tri, z_own, gate_own,
    load_sem, s1_send, s1_recv, s2_send, s2_recv, l_send, l_recv, r_send, r_recv,
):
    r = lax.axis_index("row")
    c = lax.axis_index("col")
    q = cb // rb
    ch = pair.shape[-1]

    barrier = pltpu.get_barrier_semaphore()
    for step in range(1, nrow * ncol):
        dr, dc = step // ncol, step % ncol
        pl.semaphore_signal(
            barrier,
            inc=1,
            device_id={"row": lax.rem(r + dr, nrow), "col": lax.rem(c + dc, ncol)},
            device_id_type=MESH,
        )

    moves = [
        (feats, feats_v),
        (w_atom, w_atom_v),
        (w_rows, w_rows_v),
        (w_cols, w_cols_v),
        (w_left, w_l_v.at[:, :ch]),
        (w_left_gate, w_l_v.at[:, ch:]),
        (w_right, w_r_v.at[:, :ch]),
        (w_right_gate, w_r_v.at[:, ch:]),
        (w_out_gate, w_og_v),
        (w_out, w_out_v),
        (w_up, w_up_v),
        (w_upgate, w_ug_v),
        (w_down, w_dn_v),
    ]
    loads = [pltpu.make_async_copy(a, b, load_sem.at[i]) for i, (a, b) in enumerate(moves)]
    for load in loads:
        load.start()

    loads[0].wait()
    atoms = feats_v.shape[0]
    ids = lax.broadcasted_iota(jnp.int32, (tokens, atoms), 0)
    member = (ids == atom_token[...].reshape(1, atoms)) & (atom_mask[...].reshape(1, atoms) > 0)
    member = jnp.where(member, 1.0, 0.0).astype(jnp.bfloat16)
    mine = mm(member, feats_v[...])
    part_sum[...] = mine.astype(SUM_TYPE)

    pl.semaphore_wait(barrier, nrow * ncol - 1)

    sum_copies = []
    for step in range(1, nrow):
        peer = lax.rem(r + step, nrow)
        cp = pltpu.make_async_remote_copy(
            src_ref=part_sum,
            dst_ref=recv_row.at[r],
            send_sem=s1_send.at[step],
            recv_sem=s1_recv.at[r],
            device_id={"row": peer},
            device_id_type=MESH,
        )
        cp.start()
        sum_copies.append(cp)

    own_rows = pl.ds(r * rb, rb)
    own_right = pltpu.make_async_copy(pair, right_pair.at[own_rows], r_recv.at[r])
    own_right.start()

    pair_copies = []
    local_copies = []
    for step in range(1, ncol + 1):
        target_col = lax.rem(c + step, ncol)
        for sub in range(q):
            target_row = c * q + sub
            src = pair if q == 1 else pair.at[:, pl.ds(sub * rb, rb), :]
            cp = pltpu.make_async_remote_copy(
                src_ref=src,
                dst_ref=left_pair.at[own_rows],
                send_sem=l_send.at[(step - 1) * q + sub],
                recv_sem=l_recv.at[r],
                device_id={"row": target_row, "col": target_col},
                device_id_type=MESH,
            )
            if step < ncol:
                cp.start()
                pair_copies.append(cp)
            else:
                local = pltpu.make_async_copy(src, left_pair.at[own_rows], l_recv.at[r])

                @pl.when(target_row == r)
                def _():
                    local.start()

                @pl.when(target_row != r)
                def _():
                    cp.start()

                local_copies.append((target_row, cp))
    for step in range(1, nrow):
        peer = lax.rem(r + step, nrow)
        cp = pltpu.make_async_remote_copy(
            src_ref=pair,
            dst_ref=right_pair.at[own_rows],
            send_sem=r_send.at[step],
            recv_sem=r_recv.at[r],
            device_id={"row": peer},
            device_id_type=MESH,
        )
        cp.start()
        pair_copies.append(cp)

    def wait_recv(buf, sem):
        pltpu.make_async_copy(buf, buf, sem).wait()

    total = mine
    for step in range(1, nrow):
        peer = lax.rem(r + nrow - step, nrow)
        wait_recv(recv_row.at[peer], s1_recv.at[peer])
        total = total + recv_row[peer].astype(jnp.float32)
    col_sum[...] = total.astype(SUM_TYPE)
    for step in range(1, ncol):
        peer = lax.rem(c + step, ncol)
        cp = pltpu.make_async_remote_copy(
            src_ref=col_sum,
            dst_ref=recv_col.at[c],
            send_sem=s2_send.at[step],
            recv_sem=s2_recv.at[c],
            device_id={"col": peer},
            device_id_type=MESH,
        )
        cp.start()
        sum_copies.append(cp)
    for load in loads[1:]:
        load.wait()
    for step in range(1, ncol):
        peer = lax.rem(c + ncol - step, ncol)
        wait_recv(recv_col.at[peer], s2_recv.at[peer])
        total = total + recv_col[peer].astype(jnp.float32)

    pooled = mm_split(total, w_atom_v[...])
    single = layer_norm(pooled, gain_single[...].reshape(1, -1))
    row_term[...] = mm_split(single, w_rows_v[...])
    col_term[...] = mm_split(single, w_cols_v[...])

    g_pair = gain_pair[...].reshape(1, ch)
    g_tri = gain_tri[...].reshape(1, ch)
    g_trans = gain_trans[...].reshape(1, ch)
    tri[...] = jnp.zeros_like(tri)

    def biased(src, base, cols, k, size):
        ct = col_term[cols, :]
        rows = [
            src[base + k + u].astype(jnp.float32) + (row_term[pl.ds(base + k + u, 1), :] + ct)
            for u in range(size)
        ]
        return jnp.concatenate(rows, axis=0)

    kc_left = max(1, min(rb, 192 // rb))
    kc_right = max(1, min(rb, 192 // cb))
    my_rows = pl.ds(pl.multiple_of(r * rb, 8), rb)
    my_cols = pl.ds(pl.multiple_of(c * cb, 8), cb)

    @pl.loop(0, nrow)
    def _(s):
        b = lax.rem(r + s, nrow)
        base = b * rb
        wait_recv(right_pair.at[pl.ds(base, rb)], r_recv.at[b])

        def right_chunk(n, _):
            k = n * kc_right
            z = biased(right_pair, base, my_cols, k, kc_right)
            normed = layer_norm(z, g_pair).astype(jnp.bfloat16)
            both = mm(normed, w_r_v[...])
            val = sigmoid(both[:, ch:]) * both[:, :ch]
            right_blk[pl.ds(k, kc_right)] = val.reshape(kc_right, cb, ch)

            @pl.when(s == 0)
            def _():
                z_own[pl.ds(k, kc_right)] = z.reshape(kc_right, cb, ch)
                gate = sigmoid(mm(normed, w_og_v[...]))
                gate_own[pl.ds(k, kc_right)] = gate.reshape(kc_right, cb, ch)

            return 0

        lax.fori_loop(0, rb // kc_right, right_chunk, 0)
        wait_recv(left_pair.at[pl.ds(base, rb)], l_recv.at[b])

        def left_chunk(n, _):
            k = n * kc_left
            z = biased(left_pair, base, my_rows, k, kc_left)
            normed = layer_norm(z, g_pair).astype(jnp.bfloat16)
            both = mm(normed, w_l_v[...])
            val = (sigmoid(both[:, ch:]) * both[:, :ch]).reshape(kc_left, rb, ch)
            for u in range(kc_left):
                left_blk[k + u] = val[u] * token_mask[base + k + u].astype(jnp.float32)
            return 0

        lax.fori_loop(0, rb // kc_left, left_chunk, 0)

        jb = 24 if cb % 24 == 0 else 8

        @pl.loop(0, rb // 8)
        def _(ig):
            @pl.loop(0, cb // jb)
            def _(jg):
                i0 = pl.multiple_of(ig * 8, 8)
                j0 = pl.multiple_of(jg * jb, 8)

                def step_k(k, acc):
                    rv = right_blk[k, pl.ds(j0, jb), :]
                    return tuple(
                        acc[u] + left_blk[k, pl.ds(i0 + u, 1), :] * rv for u in range(8)
                    )

                acc = tuple(tri[i0 + u, pl.ds(j0, jb), :] for u in range(8))
                acc = lax.fori_loop(0, rb, step_k, acc, unroll=4)
                for u in range(8):
                    tri[i0 + u, pl.ds(j0, jb), :] = acc[u]

    lane = lax.broadcasted_iota(jnp.int32, (cb, ch), 0)
    mask_cols = jnp.zeros((cb, ch), jnp.float32)
    for j in range(cb):
        mask_cols = jnp.where(lane == j, token_mask[c * cb + j].astype(jnp.float32), mask_cols)

    ic = max(1, min(rb, 192 // cb))
    hid = w_up_v.shape[1]

    @pl.loop(0, rb // ic)
    def _(n):
        i0 = n * ic
        weighed = jnp.concatenate(
            [
                tri[i0 + u] * (mask_cols * token_mask[r * rb + i0 + u].astype(jnp.float32))
                for u in range(ic)
            ],
            axis=0,
        )
        tri_normed = layer_norm(weighed, g_tri).astype(jnp.bfloat16)
        flat = (ic * cb, ch)
        z_second = z_own[pl.ds(i0, ic)].reshape(flat) + mm(tri_normed, w_out_v[...]) * gate_own[
            pl.ds(i0, ic)
        ].reshape(flat)
        trans_in = layer_norm(z_second, g_trans).astype(jnp.bfloat16)
        result = z_second
        half = hid // 2
        for h in range(2):
            cols = slice(h * half, (h + 1) * half)
            gate = mm(trans_in, w_ug_v[:, cols])
            up = mm(trans_in, w_up_v[:, cols])
            hidden = (gate * sigmoid(gate) * up).astype(jnp.bfloat16)
            result = result + mm(hidden, w_dn_v[cols, :])
        out[pl.ds(i0, ic)] = result.reshape(ic, cb, ch).astype(out.dtype)

    for cp in sum_copies + pair_copies:
        cp.wait_send()
    for target_row, cp in local_copies:

        @pl.when(target_row != r)
        def _():
            cp.wait_send()


def per_device(nrow, ncol, *args):
    pair, feats, token_mask = args[0], args[1], args[4]
    w_atom, w_rows, w_up = args[5], args[7], args[18]
    rb, cb, ch = pair.shape
    tokens = token_mask.shape[0]
    wide = w_atom.shape[1]
    hid = w_up.shape[1]
    bf, f32 = jnp.bfloat16, jnp.float32
    q = cb // rb
    anywhere = pl.BlockSpec(memory_space=pl.ANY)
    vmem = pl.BlockSpec(memory_space=pltpu.VMEM)
    smem = pl.BlockSpec(memory_space=pltpu.SMEM)
    specs = [anywhere] * 21
    for i in (2, 3, 6, 9, 15, 17):
        specs[i] = vmem
    specs[4] = smem
    dma = pltpu.SemaphoreType.DMA
    return pl.pallas_call(
        functools.partial(kernel, nrow, ncol, rb, cb, tokens),
        out_shape=jax.ShapeDtypeStruct(pair.shape, pair.dtype),
        in_specs=specs,
        out_specs=vmem,
        scratch_shapes=[
            pltpu.VMEM(feats.shape, bf),
            pltpu.VMEM(w_atom.shape, bf),
            pltpu.VMEM((wide, ch), bf),
            pltpu.VMEM((wide, ch), bf),
            pltpu.VMEM((ch, 2 * ch), bf),
            pltpu.VMEM((ch, 2 * ch), bf),
            pltpu.VMEM((ch, ch), bf),
            pltpu.VMEM((ch, ch), bf),
            pltpu.VMEM((ch, hid), bf),
            pltpu.VMEM((ch, hid), bf),
            pltpu.VMEM((hid, ch), bf),
            pltpu.VMEM((tokens, rb, ch), bf),
            pltpu.VMEM((tokens, cb, ch), bf),
            pltpu.VMEM((tokens, ch), SUM_TYPE),
            pltpu.VMEM((nrow, tokens, ch), SUM_TYPE),
            pltpu.VMEM((tokens, ch), SUM_TYPE),
            pltpu.VMEM((ncol, tokens, ch), SUM_TYPE),
            pltpu.VMEM((tokens, ch), f32),
            pltpu.VMEM((tokens, ch), f32),
            pltpu.VMEM((rb, rb, ch), f32),
            pltpu.VMEM((rb, cb, ch), f32),
            pltpu.VMEM((rb, cb, ch), f32),
            pltpu.VMEM((rb, cb, ch), f32),
            pltpu.VMEM((rb, cb, ch), f32),
            dma((13,)),
            dma((nrow,)),
            dma((nrow,)),
            dma((ncol,)),
            dma((ncol,)),
            dma((ncol * q,)),
            dma((nrow,)),
            dma((nrow,)),
            dma((nrow,)),
        ],
        compiler_params=pltpu.CompilerParams(
            collective_id=0, has_side_effects=True, vmem_limit_bytes=60 * 1024 * 1024
        ),
    )(*args)


def solution(mesh):
    nrow, ncol = mesh.shape["row"], mesh.shape["col"]
    placed = (
        P(("parts", "row"), "col", None),
        P(("parts", "row", "col"), None),
        P(("parts", "row", "col")),
        P(("parts", "row", "col")),
        P("parts"),
    ) + (P(),) * 16
    return jax.shard_map(
        functools.partial(per_device, nrow, ncol),
        mesh=mesh,
        in_specs=placed,
        out_specs=P(("parts", "row"), "col", None),
        check_vma=False,
    )
```

```python
import functools

import jax
import jax.numpy as jnp
from jax import lax
from jax.experimental import pallas as pl
from jax.experimental.pallas import tpu as pltpu
from jax.sharding import PartitionSpec as P

norm_epsilon = 1e-05
MESH = pl.DeviceIdType.MESH
SUM_TYPE = jnp.bfloat16


def layer_norm(values, gain_vec):
    centre = jnp.mean(values, axis=-1, keepdims=True)
    centered = values - centre
    variance = jnp.mean(centered * centered, axis=-1, keepdims=True)
    return centered * lax.rsqrt(variance + norm_epsilon) * gain_vec


def sigmoid(v):
    return 0.5 * jnp.tanh(0.5 * v) + 0.5


def mm(a, b):
    return jnp.dot(a, b, preferred_element_type=jnp.float32)


def mm_split(a, b):
    high = a.astype(jnp.bfloat16)
    low = (a - high.astype(jnp.float32)).astype(jnp.bfloat16)
    return mm(high, b) + mm(low, b)


def kernel(
    nrow, ncol, rb, cb, tokens, roomy,
    pair, feats, atom_token, atom_mask, token_mask,
    w_atom, gain_single, w_rows, w_cols, gain_pair,
    w_left, w_left_gate, w_right, w_right_gate, w_out_gate,
    gain_tri, w_out, gain_trans, w_up, w_upgate, w_down,
    out,
    feats_v, w_atom_v, w_rows_v, w_cols_v, w_l_v, w_r_v, w_og_v, w_out_v, w_up_v, w_ug_v, w_dn_v,
    blocks, part_sum, recv_col, col_sum, recv_row,
    row_term, col_term, left_blk, right_blk, z_own, gate_own, part_out, part_in,
    load_sem, s1_send, s1_recv, s2_send, s2_recv, up_send, down_send, z_recv, p_send, p_recv,
):
    r = lax.axis_index("row")
    c = lax.axis_index("col")
    q = cb // rb
    ch = pair.shape[-1]

    barrier = pltpu.get_barrier_semaphore()
    peers = [{"row": lax.rem(r + step, nrow)} for step in range(1, nrow)]
    peers += [{"col": lax.rem(c + step, ncol)} for step in range(1, ncol)]
    for peer in peers:
        pl.semaphore_signal(barrier, inc=1, device_id=peer, device_id_type=MESH)

    moves = [
        (feats, feats_v),
        (pair, blocks.at[c]),
        (w_atom, w_atom_v),
        (w_rows, w_rows_v),
        (w_cols, w_cols_v),
        (w_left, w_l_v.at[:, :ch]),
        (w_left_gate, w_l_v.at[:, ch:]),
        (w_right, w_r_v.at[:, :ch]),
        (w_right_gate, w_r_v.at[:, ch:]),
        (w_out_gate, w_og_v),
        (w_out, w_out_v),
        (w_up, w_up_v),
        (w_upgate, w_ug_v),
        (w_down, w_dn_v),
    ]
    loads = [pltpu.make_async_copy(a, b, load_sem.at[i]) for i, (a, b) in enumerate(moves)]
    for load in loads:
        load.start()

    loads[0].wait()
    atoms = feats_v.shape[0]
    ids = lax.broadcasted_iota(jnp.int32, (tokens, atoms), 0)
    member = (ids == atom_token[...].reshape(1, atoms)) & (atom_mask[...].reshape(1, atoms) > 0)
    member = jnp.where(member, 1.0, 0.0).astype(jnp.bfloat16)
    mine = mm(member, feats_v[...])
    part_sum[...] = mine.astype(SUM_TYPE)

    pl.semaphore_wait(barrier, nrow + ncol - 2)

    def wait_recv(buf, sem):
        pltpu.make_async_copy(buf, buf, sem).wait()

    copies = []
    for step in range(1, ncol):
        cp = pltpu.make_async_remote_copy(
            src_ref=part_sum,
            dst_ref=recv_col.at[c],
            send_sem=s1_send.at[step],
            recv_sem=s1_recv.at[c],
            device_id={"col": lax.rem(c + step, ncol)},
            device_id_type=MESH,
        )
        cp.start()
        copies.append(cp)

    def relay(b, way, src=None):
        return pltpu.make_async_remote_copy(
            src_ref=blocks.at[b] if src is None else src,
            dst_ref=blocks.at[b],
            send_sem=(up_send if way > 0 else down_send).at[b],
            recv_sem=z_recv.at[b],
            device_id={"col": lax.rem(c + way + ncol, ncol)},
            device_id_type=MESH,
        )

    @pl.when(c < ncol - 1)
    def _():
        relay(c, 1, pair).start()

    @pl.when(c > 0)
    def _():
        relay(c, -1, pair).start()

    def forward(s):
        @pl.when((c >= s) & (c < ncol - 1))
        def _():
            b = lax.rem(c - s + ncol, ncol)
            wait_recv(blocks.at[b], z_recv.at[b])
            relay(b, 1).start()

        @pl.when((c + s < ncol) & (c > 0))
        def _():
            b = lax.rem(c + s, ncol)
            wait_recv(blocks.at[b], z_recv.at[b])
            relay(b, -1).start()

    total = mine
    for step in range(1, ncol):
        peer = lax.rem(c + ncol - step, ncol)
        wait_recv(recv_col.at[peer], s1_recv.at[peer])
        total = total + recv_col[peer].astype(jnp.float32)
    col_sum[...] = total.astype(SUM_TYPE)
    for step in range(1, nrow):
        cp = pltpu.make_async_remote_copy(
            src_ref=col_sum,
            dst_ref=recv_row.at[r],
            send_sem=s2_send.at[step],
            recv_sem=s2_recv.at[r],
            device_id={"row": lax.rem(r + step, nrow)},
            device_id_type=MESH,
        )
        cp.start()
        copies.append(cp)
    for load in loads[1:]:
        load.wait()
    for step in range(1, nrow):
        peer = lax.rem(r + nrow - step, nrow)
        wait_recv(recv_row.at[peer], s2_recv.at[peer])
        total = total + recv_row[peer].astype(jnp.float32)
    forward(1)

    pooled = mm_split(total, w_atom_v[...])
    single = layer_norm(pooled, gain_single[...].reshape(1, -1))
    row_term[...] = mm_split(single, w_rows_v[...])
    col_term[...] = mm_split(single, w_cols_v[...])

    g_pair = gain_pair[...].reshape(1, ch)
    g_tri = gain_tri[...].reshape(1, ch)
    g_trans = gain_trans[...].reshape(1, ch)
    kc = max(1, min(rb, 192 // cb))
    jb = cb if cb <= 32 else 32

    def biased(b, k):
        ct = col_term[pl.ds(pl.multiple_of(b * cb, 8), cb), :]
        rows = [
            blocks[b, k + u].astype(jnp.float32) + (row_term[pl.ds(r * rb + k + u, 1), :] + ct)
            for u in range(kc)
        ]
        return jnp.concatenate(rows, axis=0)

    def gated(normed, weights):
        both = mm(normed, weights)
        return (sigmoid(both[:, ch:]) * both[:, :ch]).reshape(kc, cb, ch)

    def piece(target, slot):
        return pltpu.make_async_remote_copy(
            src_ref=part_out.at[slot],
            dst_ref=part_in.at[r],
            send_sem=p_send.at[target],
            recv_sem=p_recv.at[r],
            device_id={"row": target},
            device_id_type=MESH,
        )

    def partial(b):
        for sub in range(q):
            target = b * q + sub
            slot = target if roomy else sub

            @pl.loop(0, rb // 8)
            def _(ig):
                i0 = pl.multiple_of(ig * 8, 8)
                for j0 in range(0, cb, jb):

                    def step_k(k, acc):
                        rv = right_blk[k, j0 : j0 + jb, :]
                        return tuple(
                            acc[u] + left_blk[k, pl.ds(sub * rb + i0 + u, 1), :] * rv
                            for u in range(8)
                        )

                    zero = jnp.zeros((jb, ch), jnp.float32)
                    acc = lax.fori_loop(0, rb, step_k, (zero,) * 8, unroll=4)
                    for u in range(8):
                        part_out[slot, i0 + u, j0 : j0 + jb, :] = acc[u].astype(part_out.dtype)

            @pl.when(target == r)
            def _():
                part_in[r] = part_out[slot]

            @pl.when(target != r)
            def _():
                cp = piece(target, slot)
                cp.start()
                if not roomy:
                    cp.wait_send()

    @pl.loop(0, rb // kc)
    def _(n):
        k = n * kc
        z = biased(c, k)
        normed = layer_norm(z, g_pair).astype(jnp.bfloat16)
        z_own[pl.ds(k, kc)] = z.reshape(kc, cb, ch)
        left_blk[pl.ds(k, kc)] = gated(normed, w_l_v[...])
        right = gated(normed, w_r_v[...])
        for u in range(kc):
            right_blk[k + u] = right[u] * token_mask[r * rb + k + u].astype(jnp.float32)
        gate_own[pl.ds(k, kc)] = sigmoid(mm(normed, w_og_v[...])).reshape(kc, cb, ch)

    partial(c)

    @pl.loop(1, ncol)
    def _(s):
        forward(s + 1)

        @pl.loop(0, 2)
        def _(side):
            b = c + (2 * side - 1) * s

            @pl.when((b >= 0) & (b < ncol))
            def _():
                inside = lax.rem(b + ncol, ncol)

                @pl.when(((side == 0) & (c == ncol - 1)) | ((side == 1) & (c == 0)))
                def _():
                    wait_recv(blocks.at[inside], z_recv.at[inside])

                @pl.loop(0, rb // kc)
                def _(n):
                    k = n * kc
                    normed = layer_norm(biased(inside, k), g_pair).astype(jnp.bfloat16)
                    left_blk[pl.ds(k, kc)] = gated(normed, w_l_v[...])

                partial(inside)

    lane = lax.broadcasted_iota(jnp.int32, (cb, ch), 0)
    mask_cols = jnp.zeros((cb, ch), jnp.float32)
    for j in range(cb):
        mask_cols = jnp.where(lane == j, token_mask[c * cb + j].astype(jnp.float32), mask_cols)

    for step in range(1, nrow):
        peer = lax.rem(r + step, nrow)
        wait_recv(part_in.at[peer], p_recv.at[peer])

    hid = w_up_v.shape[1]

    @pl.loop(0, rb // kc)
    def _(n):
        i0 = n * kc
        rows = []
        for u in range(kc):
            row = part_in[0, i0 + u].astype(jnp.float32)
            for peer in range(1, nrow):
                row = row + part_in[peer, i0 + u].astype(jnp.float32)
            rows.append(row * (mask_cols * token_mask[r * rb + i0 + u].astype(jnp.float32)))
        tri_normed = layer_norm(jnp.concatenate(rows, axis=0), g_tri).astype(jnp.bfloat16)
        flat = (kc * cb, ch)
        z_second = z_own[pl.ds(i0, kc)].reshape(flat) + mm(tri_normed, w_out_v[...]) * gate_own[
            pl.ds(i0, kc)
        ].reshape(flat)
        trans_in = layer_norm(z_second, g_trans).astype(jnp.bfloat16)
        result = z_second
        half = hid // 2
        for h in range(2):
            cols = slice(h * half, (h + 1) * half)
            gate = mm(trans_in, w_ug_v[:, cols])
            up = mm(trans_in, w_up_v[:, cols])
            hidden = (gate * sigmoid(gate) * up).astype(jnp.bfloat16)
            result = result + mm(hidden, w_dn_v[cols, :])
        out[pl.ds(i0, kc)] = result.reshape(kc, cb, ch).astype(out.dtype)

    for cp in copies:
        cp.wait_send()
    for b in range(ncol):

        @pl.when((c >= b) & (c < ncol - 1))
        def _():
            relay(b, 1).wait_send()

        @pl.when((c <= b) & (c > 0))
        def _():
            relay(b, -1).wait_send()

    if roomy:
        for step in range(1, nrow):
            target = lax.rem(r + step, nrow)
            piece(target, target).wait_send()


def per_device(nrow, ncol, *args):
    pair, feats, token_mask = args[0], args[1], args[4]
    w_atom, w_rows, w_up = args[5], args[7], args[18]
    rb, cb, ch = pair.shape
    tokens = token_mask.shape[0]
    wide = w_atom.shape[1]
    hid = w_up.shape[1]
    bf, f32 = jnp.bfloat16, jnp.float32
    q = cb // rb
    roomy = nrow * rb * cb * ch <= 1 << 22
    anywhere = pl.BlockSpec(memory_space=pl.ANY)
    vmem = pl.BlockSpec(memory_space=pltpu.VMEM)
    smem = pl.BlockSpec(memory_space=pltpu.SMEM)
    specs = [anywhere] * 21
    for i in (2, 3, 6, 9, 15, 17):
        specs[i] = vmem
    specs[4] = smem
    dma = pltpu.SemaphoreType.DMA
    return pl.pallas_call(
        functools.partial(kernel, nrow, ncol, rb, cb, tokens, roomy),
        out_shape=jax.ShapeDtypeStruct(pair.shape, pair.dtype),
        in_specs=specs,
        out_specs=vmem,
        scratch_shapes=[
            pltpu.VMEM(feats.shape, bf),
            pltpu.VMEM(w_atom.shape, bf),
            pltpu.VMEM((wide, ch), bf),
            pltpu.VMEM((wide, ch), bf),
            pltpu.VMEM((ch, 2 * ch), bf),
            pltpu.VMEM((ch, 2 * ch), bf),
            pltpu.VMEM((ch, ch), bf),
            pltpu.VMEM((ch, ch), bf),
            pltpu.VMEM((ch, hid), bf),
            pltpu.VMEM((ch, hid), bf),
            pltpu.VMEM((hid, ch), bf),
            pltpu.VMEM((ncol, rb, cb, ch), bf),
            pltpu.VMEM((tokens, ch), SUM_TYPE),
            pltpu.VMEM((ncol, tokens, ch), SUM_TYPE),
            pltpu.VMEM((tokens, ch), SUM_TYPE),
            pltpu.VMEM((nrow, tokens, ch), SUM_TYPE),
            pltpu.VMEM((tokens, ch), f32),
            pltpu.VMEM((tokens, ch), f32),
            pltpu.VMEM((rb, cb, ch), f32),
            pltpu.VMEM((rb, cb, ch), f32),
            pltpu.VMEM((rb, cb, ch), f32),
            pltpu.VMEM((rb, cb, ch), f32),
            pltpu.VMEM((nrow if roomy else q, rb, cb, ch), bf),
            pltpu.VMEM((nrow, rb, cb, ch), bf),
            dma((14,)),
            dma((ncol,)),
            dma((ncol,)),
            dma((nrow,)),
            dma((nrow,)),
            dma((ncol,)),
            dma((ncol,)),
            dma((ncol,)),
            dma((nrow,)),
            dma((nrow,)),
        ],
        compiler_params=pltpu.CompilerParams(
            collective_id=0, has_side_effects=True, vmem_limit_bytes=60 * 1024 * 1024
        ),
    )(*args)


def solution(mesh):
    nrow, ncol = mesh.shape["row"], mesh.shape["col"]
    placed = (
        P(("parts", "row"), "col", None),
        P(("parts", "row", "col"), None),
        P(("parts", "row", "col")),
        P(("parts", "row", "col")),
        P("parts"),
    ) + (P(),) * 16
    return jax.shard_map(
        functools.partial(per_device, nrow, ncol),
        mesh=mesh,
        in_specs=placed,
        out_specs=P(("parts", "row"), "col", None),
        check_vma=False,
    )
```

```python
import functools

import jax
import jax.numpy as jnp
from jax import lax
from jax.experimental import pallas as pl
from jax.experimental.pallas import tpu as pltpu
from jax.sharding import PartitionSpec as P

norm_epsilon = 1e-05
MESH = pl.DeviceIdType.MESH
SUM_TYPE = jnp.bfloat16


def layer_norm(values, gain_vec):
    centre = jnp.mean(values, axis=-1, keepdims=True)
    centered = values - centre
    variance = jnp.mean(centered * centered, axis=-1, keepdims=True)
    return centered * lax.rsqrt(variance + norm_epsilon) * gain_vec


def sigmoid(v):
    return 0.5 * jnp.tanh(0.5 * v) + 0.5


def mm(a, b):
    return jnp.dot(a, b, preferred_element_type=jnp.float32)


def mm_split(a, b):
    high = a.astype(jnp.bfloat16)
    low = (a - high.astype(jnp.float32)).astype(jnp.bfloat16)
    return mm(high, b) + mm(low, b)


def kernel(
    nrow, ncol, rb, cb, tokens, roomy,
    pair, feats, atom_token, atom_mask, token_mask,
    w_atom, gain_single, w_rows, w_cols, gain_pair,
    w_left, w_left_gate, w_right, w_right_gate, w_out_gate,
    gain_tri, w_out, gain_trans, w_up, w_upgate, w_down,
    out,
    feats_v, w_atom_v, w_rows_v, w_cols_v, w_l_v, w_r_v, w_og_v, w_out_v, w_up_v, w_ug_v, w_dn_v,
    blocks, part_sum, recv_col, col_sum, recv_row,
    row_term, col_term, left_blk, right_blk, z_own, gate_own, part_out, part_in,
    load_sem, s1_send, s1_recv, s2_send, s2_recv, up_send, down_send, z_recv, p_send, p_recv,
):
    r = lax.axis_index("row")
    c = lax.axis_index("col")
    q = cb // rb
    ch = pair.shape[-1]

    barrier = pltpu.get_barrier_semaphore()
    peers = [{"row": lax.rem(r + step, nrow)} for step in range(1, nrow)]
    peers += [{"col": lax.rem(c + step, ncol)} for step in range(1, ncol)]
    for peer in peers:
        pl.semaphore_signal(barrier, inc=1, device_id=peer, device_id_type=MESH)

    moves = [
        (feats, feats_v),
        (pair, blocks.at[c]),
        (w_atom, w_atom_v),
        (w_rows, w_rows_v),
        (w_cols, w_cols_v),
        (w_left, w_l_v.at[:, :ch]),
        (w_left_gate, w_l_v.at[:, ch:]),
        (w_right, w_r_v.at[:, :ch]),
        (w_right_gate, w_r_v.at[:, ch:]),
        (w_out_gate, w_og_v),
        (w_out, w_out_v),
        (w_up, w_up_v),
        (w_upgate, w_ug_v),
        (w_down, w_dn_v),
    ]
    loads = [pltpu.make_async_copy(a, b, load_sem.at[i]) for i, (a, b) in enumerate(moves)]
    for load in loads:
        load.start()

    loads[0].wait()
    atoms = feats_v.shape[0]
    ids = lax.broadcasted_iota(jnp.int32, (tokens, atoms), 0)
    member = (ids == atom_token[...].reshape(1, atoms)) & (atom_mask[...].reshape(1, atoms) > 0)
    member = jnp.where(member, 1.0, 0.0).astype(jnp.bfloat16)
    mine = mm(member, feats_v[...])
    part_sum[...] = mine.astype(SUM_TYPE)

    pl.semaphore_wait(barrier, nrow + ncol - 2)

    def wait_recv(buf, sem):
        pltpu.make_async_copy(buf, buf, sem).wait()

    copies = []
    for step in range(1, nrow):
        cp = pltpu.make_async_remote_copy(
            src_ref=part_sum,
            dst_ref=recv_row.at[r],
            send_sem=s1_send.at[step],
            recv_sem=s1_recv.at[r],
            device_id={"row": lax.rem(r + step, nrow)},
            device_id_type=MESH,
        )
        cp.start()
        copies.append(cp)

    def relay(b, way, src=None):
        return pltpu.make_async_remote_copy(
            src_ref=blocks.at[b] if src is None else src,
            dst_ref=blocks.at[b],
            send_sem=(up_send if way > 0 else down_send).at[b],
            recv_sem=z_recv.at[b],
            device_id={"col": lax.rem(c + way + ncol, ncol)},
            device_id_type=MESH,
        )

    @pl.when(c < ncol - 1)
    def _():
        relay(c, 1, pair).start()

    @pl.when(c > 0)
    def _():
        relay(c, -1, pair).start()

    def forward(s):
        @pl.when((c >= s) & (c < ncol - 1))
        def _():
            b = lax.rem(c - s + ncol, ncol)
            wait_recv(blocks.at[b], z_recv.at[b])
            relay(b, 1).start()

        @pl.when((c + s < ncol) & (c > 0))
        def _():
            b = lax.rem(c + s, ncol)
            wait_recv(blocks.at[b], z_recv.at[b])
            relay(b, -1).start()

    total = mine
    for step in range(1, nrow):
        peer = lax.rem(r + nrow - step, nrow)
        wait_recv(recv_row.at[peer], s1_recv.at[peer])
        total = total + recv_row[peer].astype(jnp.float32)
    col_sum[...] = total.astype(SUM_TYPE)
    for step in range(1, ncol):
        cp = pltpu.make_async_remote_copy(
            src_ref=col_sum,
            dst_ref=recv_col.at[c],
            send_sem=s2_send.at[step],
            recv_sem=s2_recv.at[c],
            device_id={"col": lax.rem(c + step, ncol)},
            device_id_type=MESH,
        )
        cp.start()
        copies.append(cp)
    forward(1)
    for load in loads[1:]:
        load.wait()
    for step in range(1, ncol):
        peer = lax.rem(c + ncol - step, ncol)
        wait_recv(recv_col.at[peer], s2_recv.at[peer])
        total = total + recv_col[peer].astype(jnp.float32)

    pooled = mm_split(total, w_atom_v[...])
    single = layer_norm(pooled, gain_single[...].reshape(1, -1))
    row_term[...] = mm_split(single, w_rows_v[...])
    col_term[...] = mm_split(single, w_cols_v[...])

    g_pair = gain_pair[...].reshape(1, ch)
    g_tri = gain_tri[...].reshape(1, ch)
    g_trans = gain_trans[...].reshape(1, ch)
    kc = max(1, min(rb, 192 // cb))
    jb = cb if cb <= 32 else 32

    def biased(b, k):
        ct = col_term[pl.ds(pl.multiple_of(b * cb, 8), cb), :]
        rows = [
            blocks[b, k + u].astype(jnp.float32) + (row_term[pl.ds(r * rb + k + u, 1), :] + ct)
            for u in range(kc)
        ]
        return jnp.concatenate(rows, axis=0)

    def gated(normed, weights):
        both = mm(normed, weights)
        return (sigmoid(both[:, ch:]) * both[:, :ch]).reshape(kc, cb, ch)

    def piece(target, slot):
        return pltpu.make_async_remote_copy(
            src_ref=part_out.at[slot],
            dst_ref=part_in.at[r],
            send_sem=p_send.at[target],
            recv_sem=p_recv.at[r],
            device_id={"row": target},
            device_id_type=MESH,
        )

    def partial(b):
        for sub in range(q):
            target = b * q + sub
            slot = target if roomy else sub

            @pl.loop(0, rb // 8)
            def _(ig):
                i0 = pl.multiple_of(ig * 8, 8)
                for j0 in range(0, cb, jb):

                    def step_k(k, acc):
                        rv = right_blk[k, j0 : j0 + jb, :]
                        return tuple(
                            acc[u] + left_blk[k, pl.ds(sub * rb + i0 + u, 1), :] * rv
                            for u in range(8)
                        )

                    zero = jnp.zeros((jb, ch), jnp.float32)
                    acc = lax.fori_loop(0, rb, step_k, (zero,) * 8, unroll=4)
                    for u in range(8):
                        part_out[slot, i0 + u, j0 : j0 + jb, :] = acc[u].astype(part_out.dtype)

            @pl.when(target == r)
            def _():
                part_in[r] = part_out[slot]

            @pl.when(target != r)
            def _():
                cp = piece(target, slot)
                cp.start()
                if not roomy:
                    cp.wait_send()

    @pl.loop(0, rb // kc)
    def _(n):
        k = n * kc
        z = biased(c, k)
        normed = layer_norm(z, g_pair).astype(jnp.bfloat16)
        z_own[pl.ds(k, kc)] = z.reshape(kc, cb, ch)
        left_blk[pl.ds(k, kc)] = gated(normed, w_l_v[...])
        right = gated(normed, w_r_v[...])
        for u in range(kc):
            right_blk[k + u] = right[u] * token_mask[r * rb + k + u].astype(jnp.float32)
        gate_own[pl.ds(k, kc)] = sigmoid(mm(normed, w_og_v[...])).reshape(kc, cb, ch)

    partial(c)

    @pl.loop(1, ncol)
    def _(s):
        forward(s + 1)

        @pl.loop(0, 2)
        def _(side):
            b = c + (2 * side - 1) * s

            @pl.when((b >= 0) & (b < ncol))
            def _():
                inside = lax.rem(b + ncol, ncol)

                @pl.when(((side == 0) & (c == ncol - 1)) | ((side == 1) & (c == 0)))
                def _():
                    wait_recv(blocks.at[inside], z_recv.at[inside])

                @pl.loop(0, rb // kc)
                def _(n):
                    k = n * kc
                    normed = layer_norm(biased(inside, k), g_pair).astype(jnp.bfloat16)
                    left_blk[pl.ds(k, kc)] = gated(normed, w_l_v[...])

                partial(inside)

    lane = lax.broadcasted_iota(jnp.int32, (cb, ch), 0)
    mask_cols = jnp.zeros((cb, ch), jnp.float32)
    for j in range(cb):
        mask_cols = jnp.where(lane == j, token_mask[c * cb + j].astype(jnp.float32), mask_cols)

    for step in range(1, nrow):
        peer = lax.rem(r + step, nrow)
        wait_recv(part_in.at[peer], p_recv.at[peer])

    hid = w_up_v.shape[1]

    @pl.loop(0, rb // kc)
    def _(n):
        i0 = n * kc
        rows = []
        for u in range(kc):
            row = part_in[0, i0 + u].astype(jnp.float32)
            for peer in range(1, nrow):
                row = row + part_in[peer, i0 + u].astype(jnp.float32)
            rows.append(row * (mask_cols * token_mask[r * rb + i0 + u].astype(jnp.float32)))
        tri_normed = layer_norm(jnp.concatenate(rows, axis=0), g_tri).astype(jnp.bfloat16)
        flat = (kc * cb, ch)
        z_second = z_own[pl.ds(i0, kc)].reshape(flat) + mm(tri_normed, w_out_v[...]) * gate_own[
            pl.ds(i0, kc)
        ].reshape(flat)
        trans_in = layer_norm(z_second, g_trans).astype(jnp.bfloat16)
        result = z_second
        half = hid // 2
        for h in range(2):
            cols = slice(h * half, (h + 1) * half)
            gate = mm(trans_in, w_ug_v[:, cols])
            up = mm(trans_in, w_up_v[:, cols])
            hidden = (gate * sigmoid(gate) * up).astype(jnp.bfloat16)
            result = result + mm(hidden, w_dn_v[cols, :])
        out[pl.ds(i0, kc)] = result.reshape(kc, cb, ch).astype(out.dtype)

    for cp in copies:
        cp.wait_send()
    for b in range(ncol):

        @pl.when((c >= b) & (c < ncol - 1))
        def _():
            relay(b, 1).wait_send()

        @pl.when((c <= b) & (c > 0))
        def _():
            relay(b, -1).wait_send()

    if roomy:
        for step in range(1, nrow):
            target = lax.rem(r + step, nrow)
            piece(target, target).wait_send()


def per_device(nrow, ncol, *args):
    pair, feats, token_mask = args[0], args[1], args[4]
    w_atom, w_rows, w_up = args[5], args[7], args[18]
    rb, cb, ch = pair.shape
    tokens = token_mask.shape[0]
    wide = w_atom.shape[1]
    hid = w_up.shape[1]
    bf, f32 = jnp.bfloat16, jnp.float32
    q = cb // rb
    roomy = nrow * rb * cb * ch <= 1 << 22
    anywhere = pl.BlockSpec(memory_space=pl.ANY)
    vmem = pl.BlockSpec(memory_space=pltpu.VMEM)
    smem = pl.BlockSpec(memory_space=pltpu.SMEM)
    specs = [anywhere] * 21
    for i in (2, 3, 6, 9, 15, 17):
        specs[i] = vmem
    specs[4] = smem
    dma = pltpu.SemaphoreType.DMA
    return pl.pallas_call(
        functools.partial(kernel, nrow, ncol, rb, cb, tokens, roomy),
        out_shape=jax.ShapeDtypeStruct(pair.shape, pair.dtype),
        in_specs=specs,
        out_specs=vmem,
        scratch_shapes=[
            pltpu.VMEM(feats.shape, bf),
            pltpu.VMEM(w_atom.shape, bf),
            pltpu.VMEM((wide, ch), bf),
            pltpu.VMEM((wide, ch), bf),
            pltpu.VMEM((ch, 2 * ch), bf),
            pltpu.VMEM((ch, 2 * ch), bf),
            pltpu.VMEM((ch, ch), bf),
            pltpu.VMEM((ch, ch), bf),
            pltpu.VMEM((ch, hid), bf),
            pltpu.VMEM((ch, hid), bf),
            pltpu.VMEM((hid, ch), bf),
            pltpu.VMEM((ncol, rb, cb, ch), bf),
            pltpu.VMEM((tokens, ch), SUM_TYPE),
            pltpu.VMEM((ncol, tokens, ch), SUM_TYPE),
            pltpu.VMEM((tokens, ch), SUM_TYPE),
            pltpu.VMEM((nrow, tokens, ch), SUM_TYPE),
            pltpu.VMEM((tokens, ch), f32),
            pltpu.VMEM((tokens, ch), f32),
            pltpu.VMEM((rb, cb, ch), f32),
            pltpu.VMEM((rb, cb, ch), f32),
            pltpu.VMEM((rb, cb, ch), f32),
            pltpu.VMEM((rb, cb, ch), f32),
            pltpu.VMEM((nrow if roomy else q, rb, cb, ch), bf),
            pltpu.VMEM((nrow, rb, cb, ch), bf),
            dma((14,)),
            dma((nrow,)),
            dma((nrow,)),
            dma((ncol,)),
            dma((ncol,)),
            dma((ncol,)),
            dma((ncol,)),
            dma((ncol,)),
            dma((nrow,)),
            dma((nrow,)),
        ],
        compiler_params=pltpu.CompilerParams(
            collective_id=0, has_side_effects=True, vmem_limit_bytes=60 * 1024 * 1024
        ),
    )(*args)


def solution(mesh):
    nrow, ncol = mesh.shape["row"], mesh.shape["col"]
    placed = (
        P(("parts", "row"), "col", None),
        P(("parts", "row", "col"), None),
        P(("parts", "row", "col")),
        P(("parts", "row", "col")),
        P("parts"),
    ) + (P(),) * 16
    return jax.shard_map(
        functools.partial(per_device, nrow, ncol),
        mesh=mesh,
        in_specs=placed,
        out_specs=P(("parts", "row"), "col", None),
        check_vma=False,
    )
```

```python
import functools

import jax
import jax.numpy as jnp
from jax import lax
from jax.experimental import pallas as pl
from jax.experimental.pallas import tpu as pltpu
from jax.sharding import PartitionSpec as P

norm_epsilon = 1e-05
MESH = pl.DeviceIdType.MESH
SUM_TYPE = jnp.bfloat16


def layer_norm(values, gain_vec):
    centre = jnp.mean(values, axis=-1, keepdims=True)
    centered = values - centre
    variance = jnp.mean(centered * centered, axis=-1, keepdims=True)
    return centered * lax.rsqrt(variance + norm_epsilon) * gain_vec


def sigmoid(v):
    return 0.5 * jnp.tanh(0.5 * v) + 0.5


def mm(a, b):
    return jnp.dot(a, b, preferred_element_type=jnp.float32)


def mm_split(a, b):
    high = a.astype(jnp.bfloat16)
    low = (a - high.astype(jnp.float32)).astype(jnp.bfloat16)
    return mm(high, b) + mm(low, b)


def kernel(
    nrow, ncol, rb, cb, tokens, roomy,
    pair, feats, atom_token, atom_mask, token_mask,
    w_atom, gain_single, w_rows, w_cols, gain_pair,
    w_left, w_left_gate, w_right, w_right_gate, w_out_gate,
    gain_tri, w_out, gain_trans, w_up, w_upgate, w_down,
    out,
    feats_v, w_atom_v, w_rows_v, w_cols_v, w_l_v, w_r_v, w_og_v, w_out_v, w_up_v, w_ug_v, w_dn_v,
    blocks, part_sum, recv_col, col_sum, recv_row,
    row_term, col_term, left_blk, right_blk, z_own, gate_own, part_out, part_in,
    load_sem, s1_send, s1_recv, s2_send, s2_recv, up_send, down_send, z_recv, p_send, p_recv,
):
    r = lax.axis_index("row")
    c = lax.axis_index("col")
    q = cb // rb
    ch = pair.shape[-1]

    barrier = pltpu.get_barrier_semaphore()
    peers = [{"row": lax.rem(r + step, nrow)} for step in range(1, nrow)]
    peers += [{"col": lax.rem(c + step, ncol)} for step in range(1, ncol)]
    for peer in peers:
        pl.semaphore_signal(barrier, inc=1, device_id=peer, device_id_type=MESH)

    moves = [
        (feats, feats_v),
        (pair, blocks.at[c]),
        (w_atom, w_atom_v),
        (w_rows, w_rows_v),
        (w_cols, w_cols_v),
        (w_left, w_l_v.at[:, :ch]),
        (w_left_gate, w_l_v.at[:, ch:]),
        (w_right, w_r_v.at[:, :ch]),
        (w_right_gate, w_r_v.at[:, ch:]),
        (w_out_gate, w_og_v),
        (w_out, w_out_v),
        (w_up, w_up_v),
        (w_upgate, w_ug_v),
        (w_down, w_dn_v),
    ]
    loads = [pltpu.make_async_copy(a, b, load_sem.at[i]) for i, (a, b) in enumerate(moves)]
    for load in loads:
        load.start()

    loads[0].wait()
    atoms = feats_v.shape[0]
    ids = lax.broadcasted_iota(jnp.int32, (tokens, atoms), 0)
    member = (ids == atom_token[...].reshape(1, atoms)) & (atom_mask[...].reshape(1, atoms) > 0)
    member = jnp.where(member, 1.0, 0.0).astype(jnp.bfloat16)
    mine = mm(member, feats_v[...])
    part_sum[...] = mine.astype(SUM_TYPE)

    pl.semaphore_wait(barrier, nrow + ncol - 2)

    def wait_recv(buf, sem):
        pltpu.make_async_copy(buf, buf, sem).wait()

    copies = []
    for step in range(1, nrow):
        cp = pltpu.make_async_remote_copy(
            src_ref=part_sum,
            dst_ref=recv_row.at[r],
            send_sem=s1_send.at[step],
            recv_sem=s1_recv.at[r],
            device_id={"row": lax.rem(r + step, nrow)},
            device_id_type=MESH,
        )
        cp.start()
        copies.append(cp)

    def relay(b, way, src=None):
        return pltpu.make_async_remote_copy(
            src_ref=blocks.at[b] if src is None else src,
            dst_ref=blocks.at[b],
            send_sem=(up_send if way > 0 else down_send).at[b],
            recv_sem=z_recv.at[b],
            device_id={"col": lax.rem(c + way + ncol, ncol)},
            device_id_type=MESH,
        )

    @pl.when(c < ncol - 1)
    def _():
        relay(c, 1, pair).start()

    @pl.when(c > 0)
    def _():
        relay(c, -1, pair).start()

    def forward(s):
        @pl.when((c >= s) & (c < ncol - 1))
        def _():
            b = lax.rem(c - s + ncol, ncol)
            wait_recv(blocks.at[b], z_recv.at[b])
            relay(b, 1).start()

        @pl.when((c + s < ncol) & (c > 0))
        def _():
            b = lax.rem(c + s, ncol)
            wait_recv(blocks.at[b], z_recv.at[b])
            relay(b, -1).start()

    total = mine
    for step in range(1, nrow):
        peer = lax.rem(r + nrow - step, nrow)
        wait_recv(recv_row.at[peer], s1_recv.at[peer])
        total = total + recv_row[peer].astype(jnp.float32)
    col_sum[...] = total.astype(SUM_TYPE)
    for step in range(1, ncol):
        cp = pltpu.make_async_remote_copy(
            src_ref=col_sum,
            dst_ref=recv_col.at[c],
            send_sem=s2_send.at[step],
            recv_sem=s2_recv.at[c],
            device_id={"col": lax.rem(c + step, ncol)},
            device_id_type=MESH,
        )
        cp.start()
        copies.append(cp)
    forward(1)
    for load in loads[1:]:
        load.wait()
    for step in range(1, ncol):
        peer = lax.rem(c + ncol - step, ncol)
        wait_recv(recv_col.at[peer], s2_recv.at[peer])
        total = total + recv_col[peer].astype(jnp.float32)

    pooled = mm_split(total, w_atom_v[...])
    single = layer_norm(pooled, gain_single[...].reshape(1, -1))
    row_term[...] = mm_split(single, w_rows_v[...])
    col_term[...] = mm_split(single, w_cols_v[...])

    g_pair = gain_pair[...].reshape(1, ch)
    g_tri = gain_tri[...].reshape(1, ch)
    g_trans = gain_trans[...].reshape(1, ch)
    kc = max(1, min(rb, 192 // cb))
    jb = cb if cb <= 32 else 32

    def biased(b, k):
        ct = col_term[pl.ds(pl.multiple_of(b * cb, 8), cb), :]
        rows = [
            blocks[b, k + u].astype(jnp.float32) + (row_term[pl.ds(r * rb + k + u, 1), :] + ct)
            for u in range(kc)
        ]
        return jnp.concatenate(rows, axis=0)

    def gated(normed, weights):
        both = mm(normed, weights)
        return (sigmoid(both[:, ch:]) * both[:, :ch]).reshape(kc, cb, ch)

    def piece(target, slot, g):
        group = pl.ds(g * 8, 8)
        return pltpu.make_async_remote_copy(
            src_ref=part_out.at[slot, group],
            dst_ref=part_in.at[r, group],
            send_sem=p_send.at[target, g],
            recv_sem=p_recv.at[r, g],
            device_id={"row": target},
            device_id_type=MESH,
        )

    def partial(b):
        for sub in range(q):
            target = b * q + sub
            slot = target if roomy else sub

            @pl.loop(0, rb // 8)
            def _(ig):
                i0 = pl.multiple_of(ig * 8, 8)
                for j0 in range(0, cb, jb):

                    def step_k(k, acc):
                        rv = right_blk[k, j0 : j0 + jb, :]
                        return tuple(
                            acc[u] + left_blk[k, pl.ds(sub * rb + i0 + u, 1), :] * rv
                            for u in range(8)
                        )

                    zero = jnp.zeros((jb, ch), jnp.float32)
                    acc = lax.fori_loop(0, rb, step_k, (zero,) * 8, unroll=4)
                    for u in range(8):
                        part_out[slot, i0 + u, j0 : j0 + jb, :] = acc[u].astype(part_out.dtype)

                @pl.when(target == r)
                def _():
                    part_in[r, pl.ds(i0, 8)] = part_out[slot, pl.ds(i0, 8)]

                @pl.when(target != r)
                def _():
                    cp = piece(target, slot, ig)
                    cp.start()
                    if not roomy:
                        cp.wait_send()

    @pl.loop(0, rb // kc)
    def _(n):
        k = n * kc
        z = biased(c, k)
        normed = layer_norm(z, g_pair).astype(jnp.bfloat16)
        z_own[pl.ds(k, kc)] = z.reshape(kc, cb, ch)
        left_blk[pl.ds(k, kc)] = gated(normed, w_l_v[...])
        right = gated(normed, w_r_v[...])
        for u in range(kc):
            right_blk[k + u] = right[u] * token_mask[r * rb + k + u].astype(jnp.float32)
        gate_own[pl.ds(k, kc)] = sigmoid(mm(normed, w_og_v[...])).reshape(kc, cb, ch)

    partial(c)

    @pl.loop(1, ncol)
    def _(s):
        forward(s + 1)

        @pl.loop(0, 2)
        def _(side):
            b = c + (2 * side - 1) * s

            @pl.when((b >= 0) & (b < ncol))
            def _():
                inside = lax.rem(b + ncol, ncol)

                @pl.when(((side == 0) & (c == ncol - 1)) | ((side == 1) & (c == 0)))
                def _():
                    wait_recv(blocks.at[inside], z_recv.at[inside])

                @pl.loop(0, rb // kc)
                def _(n):
                    k = n * kc
                    normed = layer_norm(biased(inside, k), g_pair).astype(jnp.bfloat16)
                    left_blk[pl.ds(k, kc)] = gated(normed, w_l_v[...])

                partial(inside)

    lane = lax.broadcasted_iota(jnp.int32, (cb, ch), 0)
    mask_cols = jnp.zeros((cb, ch), jnp.float32)
    for j in range(cb):
        mask_cols = jnp.where(lane == j, token_mask[c * cb + j].astype(jnp.float32), mask_cols)

    def group_arrived(g):
        for step in range(1, nrow):
            peer = lax.rem(r + step, nrow)
            wait_recv(part_in.at[peer, pl.ds(g * 8, 8)], p_recv.at[peer, g])

    if kc != 8:
        for g in range(rb // 8):
            group_arrived(g)

    hid = w_up_v.shape[1]

    @pl.loop(0, rb // kc)
    def _(n):
        i0 = n * kc
        if kc == 8:
            group_arrived(n)
        rows = []
        for u in range(kc):
            row = part_in[0, i0 + u].astype(jnp.float32)
            for peer in range(1, nrow):
                row = row + part_in[peer, i0 + u].astype(jnp.float32)
            rows.append(row * (mask_cols * token_mask[r * rb + i0 + u].astype(jnp.float32)))
        tri_normed = layer_norm(jnp.concatenate(rows, axis=0), g_tri).astype(jnp.bfloat16)
        flat = (kc * cb, ch)
        z_second = z_own[pl.ds(i0, kc)].reshape(flat) + mm(tri_normed, w_out_v[...]) * gate_own[
            pl.ds(i0, kc)
        ].reshape(flat)
        trans_in = layer_norm(z_second, g_trans).astype(jnp.bfloat16)
        result = z_second
        half = hid // 2
        for h in range(2):
            cols = slice(h * half, (h + 1) * half)
            gate = mm(trans_in, w_ug_v[:, cols])
            up = mm(trans_in, w_up_v[:, cols])
            hidden = (gate * sigmoid(gate) * up).astype(jnp.bfloat16)
            result = result + mm(hidden, w_dn_v[cols, :])
        out[pl.ds(i0, kc)] = result.reshape(kc, cb, ch).astype(out.dtype)

    for cp in copies:
        cp.wait_send()
    for b in range(ncol):

        @pl.when((c >= b) & (c < ncol - 1))
        def _():
            relay(b, 1).wait_send()

        @pl.when((c <= b) & (c > 0))
        def _():
            relay(b, -1).wait_send()

    if roomy:
        for step in range(1, nrow):
            target = lax.rem(r + step, nrow)
            for g in range(rb // 8):
                piece(target, target, g).wait_send()


def per_device(nrow, ncol, *args):
    pair, feats, token_mask = args[0], args[1], args[4]
    w_atom, w_rows, w_up = args[5], args[7], args[18]
    rb, cb, ch = pair.shape
    tokens = token_mask.shape[0]
    wide = w_atom.shape[1]
    hid = w_up.shape[1]
    bf, f32 = jnp.bfloat16, jnp.float32
    q = cb // rb
    roomy = nrow * rb * cb * ch <= 1 << 22
    anywhere = pl.BlockSpec(memory_space=pl.ANY)
    vmem = pl.BlockSpec(memory_space=pltpu.VMEM)
    smem = pl.BlockSpec(memory_space=pltpu.SMEM)
    specs = [anywhere] * 21
    for i in (2, 3, 6, 9, 15, 17):
        specs[i] = vmem
    specs[4] = smem
    dma = pltpu.SemaphoreType.DMA
    return pl.pallas_call(
        functools.partial(kernel, nrow, ncol, rb, cb, tokens, roomy),
        out_shape=jax.ShapeDtypeStruct(pair.shape, pair.dtype),
        in_specs=specs,
        out_specs=vmem,
        scratch_shapes=[
            pltpu.VMEM(feats.shape, bf),
            pltpu.VMEM(w_atom.shape, bf),
            pltpu.VMEM((wide, ch), bf),
            pltpu.VMEM((wide, ch), bf),
            pltpu.VMEM((ch, 2 * ch), bf),
            pltpu.VMEM((ch, 2 * ch), bf),
            pltpu.VMEM((ch, ch), bf),
            pltpu.VMEM((ch, ch), bf),
            pltpu.VMEM((ch, hid), bf),
            pltpu.VMEM((ch, hid), bf),
            pltpu.VMEM((hid, ch), bf),
            pltpu.VMEM((ncol, rb, cb, ch), bf),
            pltpu.VMEM((tokens, ch), SUM_TYPE),
            pltpu.VMEM((ncol, tokens, ch), SUM_TYPE),
            pltpu.VMEM((tokens, ch), SUM_TYPE),
            pltpu.VMEM((nrow, tokens, ch), SUM_TYPE),
            pltpu.VMEM((tokens, ch), f32),
            pltpu.VMEM((tokens, ch), f32),
            pltpu.VMEM((rb, cb, ch), f32),
            pltpu.VMEM((rb, cb, ch), f32),
            pltpu.VMEM((rb, cb, ch), f32),
            pltpu.VMEM((rb, cb, ch), f32),
            pltpu.VMEM((nrow if roomy else q, rb, cb, ch), bf),
            pltpu.VMEM((nrow, rb, cb, ch), bf),
            dma((14,)),
            dma((nrow,)),
            dma((nrow,)),
            dma((ncol,)),
            dma((ncol,)),
            dma((ncol,)),
            dma((ncol,)),
            dma((ncol,)),
            dma((nrow, rb // 8)),
            dma((nrow, rb // 8)),
        ],
        compiler_params=pltpu.CompilerParams(
            collective_id=0, has_side_effects=True, vmem_limit_bytes=60 * 1024 * 1024
        ),
    )(*args)


def solution(mesh):
    nrow, ncol = mesh.shape["row"], mesh.shape["col"]
    placed = (
        P(("parts", "row"), "col", None),
        P(("parts", "row", "col"), None),
        P(("parts", "row", "col")),
        P(("parts", "row", "col")),
        P("parts"),
    ) + (P(),) * 16
    return jax.shard_map(
        functools.partial(per_device, nrow, ncol),
        mesh=mesh,
        in_specs=placed,
        out_specs=P(("parts", "row"), "col", None),
        check_vma=False,
    )
```
